512 devices in a mesh: section: 16 (over y, core), expert: 8 (over x, z_lo), dp: 4 (over z_hi).
Axes of the slice: x: 4, y: 8, z: 8 (z_hi: 4, z_lo: 2; z = z_hi * 2 + z_lo), core: 2. Of those that a mesh axis runs over, the one named last changes fastest.
Arguments:
- x_fwd: bfloat16 [16, 2048, 3584], P('section', ('expert', 'dp')), may hold values from -6 to 6
- gain: float32 [16, 3584], P('section'), may hold values from 0.5 to 1.5
- w_up: bfloat16 [16, 3584, 4096], P('section', None, ('expert', 'dp')), may hold values from -0.09375 to 0.09375
- w_down: bfloat16 [16, 4096, 3584], P('section', ('expert', 'dp')), may hold values from -0.1875 to 0.1875
- routes_f: int32 [16, 2048, 2], P('section', ('expert', 'dp')), may hold values from 0 to 3, all different within a row; in each aligned block of 64 rows (0 to 63, 64 to 127, ..., all dimensions but the last counted through in order) at most 36 rows name the same one
- probs_f: float32 [16, 2048, 2], P('section', ('expert', 'dp')), may hold values from 0.2 to 1
- act_b: bfloat16 [16, 2048, 3584], P('section', ('expert', 'dp')), may hold values from -6 to 6
- grad_b: bfloat16 [16, 2048, 3584], P('section', ('expert', 'dp')), may hold values from -6 to 6
- routes_b: int32 [16, 2048, 2], P('section', ('expert', 'dp')), may hold values from 0 to 3, all different within a row; in each aligned block of 64 rows (0 to 63, 64 to 127, ..., all dimensions but the last counted through in order) at most 36 rows name the same one
- probs_b: float32 [16, 2048, 2], P('section', ('expert', 'dp')), may hold values from 0.2 to 1
Outputs:
- next_act: bfloat16 [16, 2048, 3584], P('section', ('expert', 'dp'))
- next_grad: bfloat16 [16, 2048, 3584], P('section', ('expert', 'dp'))
- gain_grad: float32 [16, 3584], P('section')
The draws below stay inside these ranges and needn't reach their ends.
Inputs may be any that keep to these rules, and one draw needn't show every extreme that they name: `routes_f`: the 2 experts of a row differ. In each aligned block of 64 rows (the rows of one device) no expert is named by more than 36 picks, a bound that some block reaches. `routes_b`: the 2 experts of a row differ. In each aligned block of 64 rows (the rows of one device) no expert is named by more than 36 picks, a bound that some block reaches.
All inputs are finite; a program needn't handle non-finite values.
Results may differ from the reference program's by a relative error of at most 0.0053.
Values may be sent and summed in bfloat16 or wider, within the bound.
A program may use at most 128 MiB of HBM per device.

```python
import math
import jax
import jax.numpy as jnp
import numpy as np
from jax import lax

D = 3584
H = 1024
EXPERTS = 4
TOP = 2
TOK = 64
MOST = 36
SECTIONS = 16
TOKENS = 2048
N_EXPERT = 8


def shard_levels(stream_key, dims, shards, smallest, high):
    def one(axis_at, shards_of):
        draws = jax.random.uniform(jax.random.fold_in(jax.random.fold_in(stream_key, 6), axis_at), (shards_of,), jnp.float32, smallest / len(shards), high / len(shards))
        return jnp.repeat(jnp.exp(draws), dims[axis_at] // shards_of).reshape((-1,) + (1,) * (len(dims) - axis_at - 1))

    level = one(*shards[0])
    for cut in shards[1:]:
        level = level * one(*cut)
    return level


def assign_block(key, own, number, rows, number_of, top, reach, skew):
    order = jax.random.permutation(key, number_of)
    packed, common = portions_of(number_of, rows * top, reach, skew, True), portions_of(number_of, rows * top, reach, skew, False)
    places = jnp.arange(number_of)

    def named(tallies, rotation):
        used = int((tallies > 0).sum())
        fixed = max(1, used // 4)
        passed = fixed + (places - fixed + rotation * (used - fixed)) % max(1, number_of - fixed)
        return jnp.zeros((number_of,), jnp.int32).at[order[jnp.where(places < fixed, places, passed)]].set(jnp.asarray(tallies, jnp.int32))

    tallies = jnp.where(number % 4 == 0, named(packed, number // 4), named(common, number - number // 4 - 1))
    mixed = jax.random.permutation(jax.random.fold_in(own, 3), number_of)
    donor, taker = mixed[0:number_of // 2 * 2:2], mixed[1:number_of // 2 * 2:2]
    room = jnp.minimum(tallies[donor] - 1, reach - tallies[taker]) // 2
    room = jnp.where((donor == order[0]) | (taker == order[0]) | (tallies[taker] == 0), 0, jnp.maximum(room, 0))
    passed = jax.random.randint(jax.random.fold_in(own, 4), (number_of // 2,), 0, 1 << 20) % (room + 1)
    tallies = tallies.at[donor].add(-passed).at[taker].add(passed)
    labels = jnp.searchsorted(jnp.cumsum(tallies), jnp.arange(rows * top), side="right").astype(jnp.int32)
    listing = labels.reshape(top, rows).T
    listing = listing[jax.random.permutation(jax.random.fold_in(own, 1), rows)]
    rotation = jax.random.randint(jax.random.fold_in(own, 2), (rows, 1), 0, top)
    return jnp.take_along_axis(listing, (jnp.arange(top)[None, :] + rotation) % top, axis=1)


def portions_of(amount, total, most, skew, full):
    portions = [(1 << 20) // math.isqrt(rank ** skew) + 1 for rank in range(1, amount + 1)]
    largest = most if full else min(most, max(-(-total // amount), total * portions[0] // sum(portions)))
    least = 1 if total - largest >= amount - 1 else 0
    counts, spare = [largest] + [least] * (amount - 1), total - largest - least * (amount - 1)
    while spare > 0:
        free = [i for i in range(1, amount) if counts[i] < largest] or [i for i in range(1, amount) if counts[i] < most]
        whole, left = sum([portions[i] for i in free]), spare
        for i in free:
            more = min(most - counts[i], max(1, left * portions[i] // whole), spare)
            counts[i] = counts[i] + more
            spare = spare - more
    return np.array(counts)


def gaussian(stream_key, dims, scale, reach, pieces=(), dtype=jnp.bfloat16):
    loudness = shard_levels(stream_key, dims, pieces, -0.22, 0.18) if pieces else 1.0
    entries = jax.random.normal(stream_key, dims, jnp.float32) * scale * loudness
    return jnp.minimum(jnp.maximum(entries, -reach), reach).astype(dtype)


def setup_inputs(seed: int = 0) -> dict:
    key_list = jax.random.split(jax.random.key(seed), 11)
    x_fwd = gaussian(key_list[0], (SECTIONS, TOKENS, D), 1.0, 6.0, ((0, 16), (1, 32)))
    gain = jnp.clip(1.0 + 0.1 * jax.random.normal(key_list[1], (SECTIONS, D), jnp.float32), 0.5, 1.5)
    w_up = gaussian(key_list[2], (SECTIONS, D, EXPERTS * H), D ** -0.5, 0.09375, ((0, 16), (2, 32)))
    w_down = gaussian(key_list[3], (SECTIONS, EXPERTS * H, D), H ** -0.5, 0.1875, ((0, 16), (1, 32)))
    routes_f_keys = jax.random.split(jax.random.fold_in(key_list[4], 1), SECTIONS * TOKENS // TOK)
    routes_f_turns = jax.random.permutation(jax.random.fold_in(key_list[4], 3), SECTIONS * TOKENS // TOK)
    routes_f = jax.vmap(lambda own, number: assign_block(jax.random.fold_in(key_list[4], 2), own, number, TOK, EXPERTS, TOP, MOST, 2))(routes_f_keys, routes_f_turns).reshape((SECTIONS, TOKENS, TOP))
    probs_f = jnp.clip(0.2 + 0.8 * jax.random.uniform(key_list[5], (SECTIONS, TOKENS, TOP), jnp.float32) ** shard_levels(key_list[5], (SECTIONS, TOKENS, TOP), ((0, 16), (1, 32)), -0.2, 0.2), 0.2, 1.0)
    act_b = gaussian(key_list[6], (SECTIONS, TOKENS, D), 1.0, 6.0, ((0, 16), (1, 32)))
    grad_b = gaussian(key_list[7], (SECTIONS, TOKENS, D), 1.0, 6.0, ((0, 16), (1, 32)))
    routes_b_keys = jax.random.split(jax.random.fold_in(key_list[8], 1), SECTIONS * TOKENS // TOK)
    routes_b_turns = jax.random.permutation(jax.random.fold_in(key_list[8], 3), SECTIONS * TOKENS // TOK)
    routes_b = jax.vmap(lambda own, number: assign_block(jax.random.fold_in(key_list[8], 2), own, number, TOK, EXPERTS, TOP, MOST, 2))(routes_b_keys, routes_b_turns).reshape((SECTIONS, TOKENS, TOP))
    probs_b = jnp.clip(0.2 + 0.8 * jax.random.uniform(key_list[9], (SECTIONS, TOKENS, TOP), jnp.float32) ** shard_levels(key_list[9], (SECTIONS, TOKENS, TOP), ((0, 16), (1, 32)), -0.2, 0.2), 0.2, 1.0)
    return dict(x_fwd=x_fwd, gain=gain, w_up=w_up, w_down=w_down, routes_f=routes_f, probs_f=probs_f, act_b=act_b, grad_b=grad_b, routes_b=routes_b, probs_b=probs_b)


EPS = 1e-06

def apply_norm(rows, gain_gradient_row):
    wide_hidden = rows.astype(jnp.float32)
    inverse_scale = lax.rsqrt(lax.optimization_barrier(jnp.mean(wide_hidden * wide_hidden, axis=-1, keepdims=True)) + EPS)
    unit_rows = wide_hidden * inverse_scale
    return (unit_rows, inverse_scale, (unit_rows * gain_gradient_row).astype(jnp.bfloat16))

def section_step(items):
    input_rows, gain_gradient_row, up, down, rf, pf, activation_back_rows, gradient_back_rows, rb, pb = items
    parts = max(1, N_EXPERT // EXPERTS)
    width = H // parts
    forward_unit_rows, forward_scale, normed_forward_rows = apply_norm(input_rows, gain_gradient_row)
    backward_unit_rows, backward_scale, normed_backward_rows = apply_norm(activation_back_rows, gain_gradient_row)
    mixed = jnp.zeros(input_rows.shape, jnp.float32)
    gradient_list = jnp.zeros(input_rows.shape, jnp.float32)
    for expert_index in range(EXPERTS):
        up_e = up[:, expert_index * H:(expert_index + 1) * H]
        down_e = down[expert_index * H:(expert_index + 1) * H, :]
        weight_f = lax.optimization_barrier(jnp.sum(pf * (rf == expert_index).astype(jnp.float32), axis=1))
        weight_b = lax.optimization_barrier(jnp.sum(pb * (rb == expert_index).astype(jnp.float32), axis=1))
        pre = jnp.dot(normed_forward_rows, up_e, preferred_element_type=jnp.float32)
        hidden_state = jax.nn.silu(pre).astype(jnp.bfloat16)
        out_e = jnp.zeros(input_rows.shape, jnp.float32)
        for part in range(parts):
            cut = slice(part * width, (part + 1) * width)
            piece = jnp.dot(hidden_state[:, cut], down_e[cut, :], preferred_element_type=jnp.float32)
            out_e = out_e + piece.astype(jnp.bfloat16).astype(jnp.float32)
        mixed = mixed + weight_f[:, None] * out_e
        pre_b = jnp.dot(normed_backward_rows, up_e, preferred_element_type=jnp.float32)
        hidden_gradient = jnp.dot(gradient_back_rows, down_e.T, preferred_element_type=jnp.float32)
        sig = jax.nn.sigmoid(pre_b)
        dpre = (hidden_gradient * sig * (1.0 + pre_b * (1.0 - sig))).astype(jnp.bfloat16)
        dn_e = jnp.zeros(input_rows.shape, jnp.float32)
        for part in range(parts):
            cut = slice(part * width, (part + 1) * width)
            piece = jnp.dot(dpre[:, cut], up_e[:, cut].T, preferred_element_type=jnp.float32)
            dn_e = dn_e + piece.astype(jnp.bfloat16).astype(jnp.float32)
        gradient_list = gradient_list + weight_b[:, None] * dn_e
    result = (input_rows.astype(jnp.float32) + mixed).astype(jnp.bfloat16)
    gain_gradient_part = lax.optimization_barrier(jnp.sum(gradient_list * backward_unit_rows, axis=0))
    scaled_rows = gradient_list * gain_gradient_row
    input_gradient = gradient_back_rows.astype(jnp.float32) + backward_scale * (scaled_rows - backward_unit_rows * lax.optimization_barrier(jnp.mean(scaled_rows * backward_unit_rows, axis=-1, keepdims=True)))
    return (result, input_gradient.astype(jnp.bfloat16), gain_gradient_part)

def reference(x_fwd, gain, w_up, w_down, routes_f, probs_f, act_b, grad_b, routes_b, probs_b):
    result, input_gradient, gain_grad = lax.map(section_step, (x_fwd, gain, w_up, w_down, routes_f, probs_f, act_b, grad_b, routes_b, probs_b))
    next_act = jnp.roll(result, 1, axis=0)
    next_grad = jnp.roll(input_gradient, -1, axis=0)
    return (next_act, next_grad, gain_grad)
```

```python
import functools

import jax
import jax.numpy as jnp
from jax import lax
from jax.experimental import pallas as pl
from jax.experimental.pallas import tpu as pltpu
from jax.sharding import PartitionSpec as P

EXPERTS = 4
MOST = 36
EPS = 1e-06
ROWS = 48
CHUNKS = 4
LANES = 256
TOKEN_STEP = 3
MESH = pl.DeviceIdType.MESH
F32 = jnp.float32
BF16 = jnp.bfloat16


def nt(a, b):
    return lax.dot_general(a, b, (((1,), (1,)), ((), ())), preferred_element_type=F32)


def tn(a, b):
    return lax.dot_general(a, b, (((0,), (0,)), ((), ())), preferred_element_type=F32)


def nn(a, b):
    return jnp.dot(a, b, preferred_element_type=F32)


def relay(
    dims,
    x_ref, gain_ref, up_in, down_in, rf_ref, pf_ref, act_ref, g_ref, rb_ref, pb_ref,
    act_out, grad_out, gain_out,
    up, down, packs, tok_n, tok_g, pre, hid, dh, out_acc, ret_f, ret_b, back_f, back_b,
    x_in, act_in, g_in, gain_in, wf, wb, wf_in, wb_in, qg, gpart, gx, gz_own, gz,
    z_send, z_recv, own_sem, t_send, t_recv, f_send, f_recv, b_send, b_recv,
    s_send, s_recv, gx_send, gx_recv, gz_send, gz_recv,
):
    sections, nz, zlo = dims
    tokens, width = x_ref.shape
    wide = width // CHUNKS
    used = EXPERTS * ROWS
    s, e, d = lax.axis_index("section"), lax.axis_index("expert"), lax.axis_index("dp")
    x, z = e // zlo, d * zlo + e % zlo
    nxt, prv = lax.rem(s + 1, sections), lax.rem(s + sections - 1, sections)
    sign = 1 - 2 * lax.rem(s, 2)
    reach_a, reach_b = nz // 2, nz // 2 - 1

    def place(section, xx, zz):
        return (section, xx * zlo + lax.rem(zz, zlo), zz // zlo)

    def at_x(k):
        return lax.rem(x + k + EXPERTS, EXPERTS)

    def at_z(k):
        return lax.rem(z + k + nz, nz)

    peers = [place(s, at_x(k), z) for k in range(1, EXPERTS)]
    peers += [place(s, x, at_z(k)) for k in range(1, nz)]
    peers += [place(nxt, at_x(k), z) for k in range(EXPERTS)]
    peers += [place(prv, at_x(k), z) for k in range(EXPERTS)]
    barrier = pltpu.get_barrier_semaphore()
    for peer in peers:
        pl.semaphore_signal(barrier, inc=1, device_id=peer, device_id_type=MESH)
    pl.semaphore_wait(barrier, len(peers))

    sent = []

    def send(src, dst, send_sem, recv_sem, device):
        copy = pltpu.make_async_remote_copy(
            src_ref=src, dst_ref=dst, send_sem=send_sem, recv_sem=recv_sem,
            device_id=device, device_id_type=MESH,
        )
        copy.start()
        sent.append(copy)
        return copy

    long_way, short_way = place(s, x, at_z(sign)), place(s, x, at_z(-sign))
    moving = {}

    def own_piece(c):
        if c < CHUNKS:
            return up_in.at[c]
        return down_in.at[:, pl.ds((c - CHUNKS) * wide, wide)]

    def held(slot, c):
        return up.at[slot, c] if c < CHUNKS else down.at[slot, c - CHUNKS]

    def pass_on(c, frm, to, device):
        src = own_piece(c) if frm == 0 else held(frm, c)
        moving[c, to] = send(
            src, held(to, c), z_send.at[c, to - 1], z_recv.at[c, to - 1], device
        )

    def start_own(c):
        pass_on(c, 0, 1, long_way)
        pass_on(c, 0, reach_a + 1, short_way)

    def pass_round(c, r):
        moving[c, r].wait_recv()
        if r < reach_a:
            pass_on(c, r, r + 1, long_way)
        if r <= reach_b:
            moving[c, reach_a + r].wait_recv()
            if r < reach_b:
                pass_on(c, reach_a + r, reach_a + r + 1, short_way)

    start_own(0)
    start_own(1)
    start_own(2)
    keep = [pltpu.make_async_copy(own_piece(c), held(0, c), own_sem.at[c]) for c in range(2 * CHUNKS)]
    for copy in keep:
        copy.start()

    ahead, behind = place(nxt, x, z), place(prv, x, z)
    arriving = {}
    arriving["x"] = send(x_ref, x_in, s_send.at[0], s_recv.at[0], ahead)
    arriving["act"] = send(act_ref, act_in, s_send.at[1], s_recv.at[1], behind)
    arriving["g"] = send(g_ref, g_in, s_send.at[2], s_recv.at[2], behind)
    arriving["gain"] = send(gain_ref, gain_in, s_send.at[3], s_recv.at[3], behind)

    column = lax.broadcasted_iota(jnp.int32, (tokens, LANES), 1)
    block = sum((column >= k * ROWS).astype(jnp.int32) for k in range(1, EXPERTS))
    slot = (column - block * ROWS).astype(F32)
    expert = x + block
    expert = jnp.where(expert >= EXPERTS, expert - EXPERTS, expert)
    earlier = (
        lax.broadcasted_iota(jnp.int32, (tokens, tokens), 1)
        < lax.broadcasted_iota(jnp.int32, (tokens, tokens), 0)
    ).astype(F32).astype(BF16)

    def layout(r_ref, p_ref):
        first, second = r_ref[:, 0:1] == expert, r_ref[:, 1:2] == expert
        chosen = jnp.where(first | second, 1.0, 0.0)
        before = nn(earlier, chosen.astype(BF16))
        taken = (before == slot) & (chosen > 0.5) & (column < used)
        weight = jnp.where(first, p_ref[:, 0:1], 0.0) + jnp.where(second, p_ref[:, 1:2], 0.0)
        return jnp.where(taken, 1.0, 0.0).astype(BF16)[:, :used], jnp.where(taken, weight, 0.0)

    pick_b, weight_b = layout(rb_ref, pb_ref)
    pick_f, weight_f = layout(rf_ref, pf_ref)
    wf[...] = weight_f
    wb[...] = weight_b
    arriving["wf"] = send(wf, wf_in, s_send.at[4], s_recv.at[4], ahead)
    arriving["wb"] = send(wb, wb_in, s_send.at[5], s_recv.at[5], behind)

    def part(ref, c):
        return ref[:, c * wide:(c + 1) * wide]

    def scale_of(ref):
        total = jnp.zeros((tokens, 1), F32)
        for c in range(CHUNKS):
            v = part(ref, c).astype(F32)
            total = total + jnp.sum(v * v, axis=-1, keepdims=True)
        return lax.rsqrt(total / width + EPS)

    def distribute(index, pick, rows_of, kept, base):
        for c in range(CHUNKS):
            rows = tn(pick, rows_of(c)).astype(BF16)
            packs[index, c] = rows
            kept[c, base:base + ROWS, :] = rows[:ROWS]
        for k in range(1, EXPERTS):
            n = index * (EXPERTS - 1) + k - 1
            arriving["tok", index, k] = send(
                packs.at[index, :, pl.ds(k * ROWS, ROWS), :],
                kept.at[:, pl.ds(base + k * ROWS, ROWS), :],
                t_send.at[n], t_recv.at[n], place(s, at_x(k), z),
            )

    def normed(ref):
        scale = scale_of(ref)
        return lambda c: (part(ref, c).astype(F32) * scale * part(gain_ref, c)).astype(BF16)

    distribute(0, pick_f, normed(x_ref), tok_n, 0)
    distribute(1, pick_b, normed(act_ref), tok_n, used)
    distribute(2, pick_b, lambda c: part(g_ref, c), tok_g, 0)
    for copy in keep:
        copy.wait()

    def tokens_of(index):
        for k in range(1, EXPERTS):
            arriving["tok", index, k].wait_recv()

    def both(ref, pair, c, axis):
        one, other = (0, reach_a) if pair == 0 else (pair, reach_a + pair)
        return jnp.concatenate([ref[one, c], ref[other, c]], axis=axis)

    def up_piece(c, pair, step):
        term = nn(tok_n[c], both(up, pair, c, 1))
        if c == 0:
            pre[pair] = term
        else:
            pre[pair] += term
        if c == CHUNKS - 1:
            v = pre[pair, :used, :]
            hid[pair] = (v * jax.nn.sigmoid(v)).astype(BF16)

    def down_piece(c, pair, step):
        block_of = both(down, pair, c, 0)
        term = nt(tok_g[c], block_of)
        if c == 0:
            dh[pair] = term
        else:
            dh[pair] += term
        term = nn(hid[pair], block_of)
        if pair == 1 % (nz // 2):
            out_acc[c] = term
        elif pair != 0:
            out_acc[c] += term
        else:
            ret_f[c] = (out_acc[c] + term).astype(BF16)
            give_back("f", c, ret_f, back_f, f_send, f_recv, nxt)

    def give_back(name, c, src, dst, send_sem, recv_sem, section):
        for k in range(EXPERTS):
            rows = pl.ds(k * ROWS, ROWS)
            arriving[name, c, k] = send(
                src.at[c, rows, :], dst.at[c, rows, :],
                send_sem.at[c, k], recv_sem.at[c, k], place(section, at_x(-k), z),
            )

    waiting = []
    have_n = have_g = False
    for t in range(1, 2 * CHUNKS + reach_a):
        if 3 <= t + 1 < 2 * CHUNKS:
            start_own(t + 1)
        for r in range(1, reach_a + 1):
            c = t - r
            if 0 <= c < 2 * CHUNKS:
                pass_round(c, r)
                waiting.append((c, r % reach_a))
        if t >= TOKEN_STEP:
            if not have_n:
                tokens_of(0)
                tokens_of(1)
                have_n = True
            for c, pair in waiting:
                if c < CHUNKS:
                    up_piece(c, pair, t)
                else:
                    if not have_g:
                        tokens_of(2)
                        have_g = True
                    down_piece(c - CHUNKS, pair, t)
            waiting = []

    dpre = []
    for pair in range(nz // 2):
        v = pre[pair, used:, :]
        sig = jax.nn.sigmoid(v)
        dpre.append((dh[pair] * sig * (1.0 + v * (1.0 - sig))).astype(BF16))
    for c in range(CHUNKS):
        total = nt(dpre[0], both(up, 0, c, 1))
        for pair in range(1, nz // 2):
            total = total + nt(dpre[pair], both(up, pair, c, 1))
        ret_b[c] = total.astype(BF16)
        give_back("b", c, ret_b, back_b, b_send, b_recv, prv)

    def gathered(weights, back, c):
        w = weights[:, :used]
        high = w.astype(BF16)
        low = (w - high.astype(F32)).astype(BF16)
        return nn(high, back[c]) + nn(low, back[c])

    arriving["x"].wait_recv()
    arriving["wf"].wait_recv()
    for c in range(CHUNKS):
        for k in range(EXPERTS):
            arriving["f", c, k].wait_recv()
        mixed = gathered(wf_in, back_f, c)
        act_out[:, c * wide:(c + 1) * wide] = (part(x_in, c).astype(F32) + mixed).astype(BF16)

    for name in ("act", "g", "gain", "wb"):
        arriving[name].wait_recv()
    scale = scale_of(act_in)
    dot = jnp.zeros((tokens, 1), F32)
    for c in range(CHUNKS):
        for k in range(EXPERTS):
            arriving["b", c, k].wait_recv()
        q = gathered(wb_in, back_b, c)
        xhat = part(act_in, c).astype(F32) * scale
        gpart[:, c * wide:(c + 1) * wide] = jnp.sum(q * xhat, axis=0, keepdims=True)
        scaled = q * part(gain_in, c)
        qg[c] = scaled
        dot = dot + jnp.sum(scaled * xhat, axis=-1, keepdims=True)
    for k in range(EXPERTS):
        arriving["gx", k] = send(
            gpart, gx.at[x], gx_send.at[k], gx_recv.at[x], place(nxt, at_x(k), z)
        )
    mean = dot / width
    for c in range(CHUNKS):
        xhat = part(act_in, c).astype(F32) * scale
        dx = part(g_in, c).astype(F32) + scale * (qg[c] - xhat * mean)
        grad_out[:, c * wide:(c + 1) * wide] = dx.astype(BF16)
    for k in range(EXPERTS):
        pltpu.make_async_remote_copy(
            src_ref=gpart, dst_ref=gx.at[k], send_sem=gx_send.at[k], recv_sem=gx_recv.at[k],
            device_id=ahead, device_id_type=MESH,
        ).wait_recv()
    total = gx[0]
    for k in range(1, EXPERTS):
        total = total + gx[k]
    gz_own[...] = total
    gz[z] = total
    for k in range(1, nz):
        send(gz_own, gz.at[z], gz_send.at[k - 1], gz_recv.at[z], place(s, x, at_z(k)))
    for k in range(1, nz):
        frm = at_z(k)
        pltpu.make_async_remote_copy(
            src_ref=gz_own, dst_ref=gz.at[frm], send_sem=gz_send.at[k - 1],
            recv_sem=gz_recv.at[frm], device_id=long_way, device_id_type=MESH,
        ).wait_recv()
    total = gz[0]
    for k in range(1, nz):
        total = total + gz[k]
    gain_out[...] = total
    for copy in sent:
        copy.wait_send()


def body(sections, ranks, dp, x_fwd, gain, w_up, w_down, routes_f, probs_f, act_b, grad_b, routes_b, probs_b):
    zlo = ranks // EXPERTS
    nz = zlo * dp
    tokens, width = x_fwd.shape[1:]
    wide = width // CHUNKS
    hidden = w_up.shape[-1]
    used = EXPERTS * ROWS
    pairs = nz // 2
    vmem, anywhere = pl.BlockSpec(memory_space=pltpu.VMEM), pl.BlockSpec(memory_space=pl.ANY)
    dma = pltpu.SemaphoreType.DMA
    scratch = [
        pltpu.VMEM((nz, CHUNKS, wide, hidden), BF16),
        pltpu.VMEM((nz, CHUNKS, hidden, wide), BF16),
        pltpu.VMEM((3, CHUNKS, used, wide), BF16),
        pltpu.VMEM((CHUNKS, 2 * used, wide), BF16),
        pltpu.VMEM((CHUNKS, used, wide), BF16),
        pltpu.VMEM((pairs, 2 * used, 2 * hidden), F32),
        pltpu.VMEM((pairs, used, 2 * hidden), BF16),
        pltpu.VMEM((pairs, used, 2 * hidden), F32),
        pltpu.VMEM((CHUNKS, used, wide), F32),
        pltpu.VMEM((CHUNKS, used, wide), BF16),
        pltpu.VMEM((CHUNKS, used, wide), BF16),
        pltpu.VMEM((CHUNKS, used, wide), BF16),
        pltpu.VMEM((CHUNKS, used, wide), BF16),
        pltpu.VMEM((tokens, width), BF16),
        pltpu.VMEM((tokens, width), BF16),
        pltpu.VMEM((tokens, width), BF16),
        pltpu.VMEM((1, width), F32),
        pltpu.VMEM((tokens, LANES), F32),
        pltpu.VMEM((tokens, LANES), F32),
        pltpu.VMEM((tokens, LANES), F32),
        pltpu.VMEM((tokens, LANES), F32),
        pltpu.VMEM((CHUNKS, tokens, wide), F32),
        pltpu.VMEM((1, width), F32),
        pltpu.VMEM((EXPERTS, 1, width), F32),
        pltpu.VMEM((1, width), F32),
        pltpu.VMEM((nz, 1, width), F32),
        dma((2 * CHUNKS, nz - 1)), dma((2 * CHUNKS, nz - 1)), dma((2 * CHUNKS,)),
        dma((3 * (EXPERTS - 1),)), dma((3 * (EXPERTS - 1),)),
        dma((CHUNKS, EXPERTS)), dma((CHUNKS, EXPERTS)),
        dma((CHUNKS, EXPERTS)), dma((CHUNKS, EXPERTS)),
        dma((6,)), dma((6,)),
        dma((EXPERTS,)), dma((EXPERTS,)), dma((nz - 1,)), dma((nz,)),
    ]
    act, grad, gain_grad = pl.pallas_call(
        functools.partial(relay, (sections, nz, zlo)),
        out_shape=(
            jax.ShapeDtypeStruct((tokens, width), BF16),
            jax.ShapeDtypeStruct((tokens, width), BF16),
            jax.ShapeDtypeStruct((1, width), F32),
        ),
        in_specs=[vmem, vmem, anywhere, anywhere] + [vmem] * 6,
        out_specs=(vmem, vmem, vmem),
        scratch_shapes=scratch,
        compiler_params=pltpu.CompilerParams(
            collective_id=0, has_side_effects=True, vmem_limit_bytes=52 * 2**20
        ),
    )(
        x_fwd[0], gain, w_up.reshape(CHUNKS, wide, hidden), w_down[0],
        routes_f[0], probs_f[0], act_b[0], grad_b[0], routes_b[0], probs_b[0],
    )
    return act[None], grad[None], gain_grad


def solution(mesh):
    sizes = mesh.shape
    rows, weights = P("section", ("expert", "dp"), None), P("section", None, ("expert", "dp"))
    return jax.shard_map(
        functools.partial(body, sizes["section"], sizes["expert"], sizes["dp"]),
        mesh=mesh,
        in_specs=(rows, P("section", None), weights) + (rows,) * 7,
        out_specs=(rows, rows, P("section", None)),
        check_vma=False,
    )
```

```python
import functools

import jax
import jax.numpy as jnp
from jax import lax
from jax.experimental import pallas as pl
from jax.experimental.pallas import tpu as pltpu
from jax.sharding import PartitionSpec as P

EXPERTS = 4
EPS = 1e-06
MAIN = 32
REST = 4
SLOTS = EXPERTS * (MAIN + REST)
MAINS = EXPERTS * MAIN
LANE = 128
PIECE = LANE * MAIN // REST
FINE = PIECE // 2
TOKEN_STEP = 4
MESH = pl.DeviceIdType.MESH
F32 = jnp.float32
BF16 = jnp.bfloat16


def nt(a, b):
    return lax.dot_general(a, b, (((1,), (1,)), ((), ())), preferred_element_type=F32)


def tn(a, b):
    return lax.dot_general(a, b, (((0,), (0,)), ((), ())), preferred_element_type=F32)


def nn(a, b):
    return jnp.dot(a, b, preferred_element_type=F32)


def cuts(width, piece=PIECE):
    return [(at, min(piece, width - at)) for at in range(0, width, piece)]


def relay(
    dims,
    x_hbm, gain_hbm, up_in, down_in, rf_hbm, pf_hbm, act_hbm, g_hbm, rb_hbm, pb_hbm,
    act_out, grad_out, gain_out,
    x_ref, gain_ref, rf_ref, pf_ref, act_ref, g_ref, rb_ref, pb_ref,
    up, down, packs, tok, rest, pre, hid, dh, dpre, out_acc, dn_acc, ret_f, ret_b, back_f, back_b,
    x_in, act_in, g_in, gain_in, wf, wb, wf_in, wb_in, qg, gpart, gz, gx_own, gx,
    in_sem, own_sem, z_send, z_recv, t_send, t_recv, f_send, f_recv, b_send, b_recv,
    s_send, s_recv, gx_send, gx_recv, gz_send, gz_recv,
):
    sections, nz, zlo = dims
    tokens, width = x_ref.shape
    parts = cuts(width)
    pieces = len(parts)
    fine = cuts(width, FINE)
    fines = len(fine)
    all_cuts = parts + fine
    last = len(all_cuts)
    pairs = nz // 2
    s, e, d = lax.axis_index("section"), lax.axis_index("expert"), lax.axis_index("dp")
    x, z = e // zlo, d * zlo + e % zlo
    nxt, prv = lax.rem(s + 1, sections), lax.rem(s + sections - 1, sections)
    sign = 1 - 2 * lax.rem(s, 2)
    reach_a, reach_b = nz // 2, nz // 2 - 1

    def place(section, xx, zz):
        return (section, xx * zlo + lax.rem(zz, zlo), zz // zlo)

    def at_x(k):
        return lax.rem(x + k + EXPERTS, EXPERTS)

    def at_z(k):
        return lax.rem(z + k + nz, nz)

    peers = [place(s, x, at_z(k)) for k in range(1, nz)]
    peers += [place(s, at_x(k), z) for k in range(1, EXPERTS)]
    peers += [place(nxt, at_x(k), z) for k in range(EXPERTS)]
    peers += [place(prv, at_x(k), z) for k in range(EXPERTS)]
    barrier = pltpu.get_barrier_semaphore()
    for peer in peers:
        pl.semaphore_signal(barrier, inc=1, device_id=peer, device_id_type=MESH)
    fetched = [
        (rf_hbm, rf_ref), (rb_hbm, rb_ref), (pf_hbm, pf_ref), (pb_hbm, pb_ref), (gain_hbm, gain_ref),
        (x_hbm, x_ref), (act_hbm, act_ref), (g_hbm, g_ref),
    ]
    fetched = [pltpu.make_async_copy(a, b, in_sem.at[i]) for i, (a, b) in enumerate(fetched)]
    for copy in fetched:
        copy.start()
    pl.semaphore_wait(barrier, len(peers))

    sent = []

    def send(src, dst, send_sem, recv_sem, device):
        copy = pltpu.make_async_remote_copy(
            src_ref=src, dst_ref=dst, send_sem=send_sem, recv_sem=recv_sem,
            device_id=device, device_id_type=MESH,
        )
        copy.start()
        sent.append(copy)
        return copy

    long_way, short_way = place(s, x, at_z(sign)), place(s, x, at_z(-sign))
    moving = {}

    def own_piece(c):
        at, size = all_cuts[c]
        return up_in.at[pl.ds(at, size), :] if c < pieces else down_in.at[:, pl.ds(at, size)]

    def held(slot, c):
        at, size = all_cuts[c]
        return up.at[slot, pl.ds(at, size), :] if c < pieces else down.at[slot, :, pl.ds(at, size)]

    def pass_on(c, frm, to, device):
        src = own_piece(c) if frm == 0 else held(frm, c)
        moving[c, to] = send(
            src, held(to, c), z_send.at[c, to - 1], z_recv.at[c, to - 1], device
        )

    def start_own(c):
        pass_on(c, 0, 1, long_way)
        pass_on(c, 0, reach_a + 1, short_way)

    def pass_round(c, r):
        moving[c, r].wait_recv()
        if r < reach_a:
            pass_on(c, r, r + 1, long_way)
        if r <= reach_b:
            moving[c, reach_a + r].wait_recv()
            if r < reach_b:
                pass_on(c, reach_a + r, reach_a + r + 1, short_way)

    for c in range(3):
        start_own(c)
    keep = [pltpu.make_async_copy(up_in, up.at[0], own_sem.at[0]), pltpu.make_async_copy(down_in, down.at[0], own_sem.at[1])]
    for copy in keep:
        copy.start()
    for copy in fetched:
        copy.wait()

    ahead, behind = place(nxt, x, z), place(prv, x, z)
    arriving = {}

    row = lax.broadcasted_iota(jnp.int32, (SLOTS, tokens), 0)
    main = row < MAINS
    block = jnp.where(main, row // MAIN, (row - MAINS) // REST)
    slot = jnp.where(main, row % MAIN, MAIN + (row - MAINS) % REST).astype(F32)
    expert = x + block
    expert = jnp.where(expert >= EXPERTS, expert - EXPERTS, expert)
    earlier = (
        lax.broadcasted_iota(jnp.int32, (tokens, tokens), 0)
        < lax.broadcasted_iota(jnp.int32, (tokens, tokens), 1)
    ).astype(F32).astype(BF16)

    def layout(r_ref, p_ref):
        first, second = r_ref[0:1, :] == expert, r_ref[1:2, :] == expert
        chosen = jnp.where(first | second, 1.0, 0.0)
        before = nn(chosen.astype(BF16), earlier)
        taken = (before == slot) & (chosen > 0.5)
        weight = jnp.where(first, p_ref[0:1, :], 0.0) + jnp.where(second, p_ref[1:2, :], 0.0)
        return jnp.where(taken, 1.0, 0.0).astype(BF16), jnp.where(taken, weight, 0.0)

    def two(w):
        high = w.astype(BF16)
        return high, (w - high.astype(F32)).astype(BF16)

    def rest_out(tiles):
        a = lax.broadcasted_iota(jnp.int32, (MAINS, tiles * EXPERTS * REST), 0)
        b = lax.broadcasted_iota(jnp.int32, (MAINS, tiles * EXPERTS * REST), 1)
        source = (a % MAIN // REST) * (EXPERTS * REST) + (a // MAIN) * REST + a % REST
        return jnp.where(source == b, 1.0, 0.0).astype(BF16)

    moves = {size // LANE: rest_out(size // LANE) for _, size in all_cuts}

    def fold(rows, size):
        tiles = size // LANE
        stack = jnp.concatenate([rows[:, i * LANE:(i + 1) * LANE] for i in range(tiles)], axis=0)
        return nn(moves[tiles], stack).astype(BF16)

    def unfold(message, size):
        tiles, deep = size // LANE, EXPERTS * REST
        stack = tn(moves[tiles], message).astype(BF16)
        return jnp.concatenate([stack[i * deep:(i + 1) * deep] for i in range(tiles)], axis=1)

    def part(ref, c):
        at, size = parts[c]
        return ref[:, at:at + size]

    def scale_of(ref):
        total = jnp.zeros((tokens, 1), F32)
        for c in range(pieces):
            v = part(ref, c).astype(F32)
            total = total + jnp.sum(v * v, axis=-1, keepdims=True)
        return lax.rsqrt(total / width + EPS)

    def distribute(index, rows_of):
        for c, (at, size) in enumerate(parts):
            rows = rows_of(c).astype(BF16)
            low = fold(rows[MAINS:], size)
            tail = width + c * LANE
            packs[index, :, at:at + size] = rows[:MAINS]
            packs[index, :, tail:tail + LANE] = low
            tok[index, :MAIN, at:at + size] = rows[:MAIN]
            tok[index, :MAIN, tail:tail + LANE] = low[:MAIN]
        for k in range(1, EXPERTS):
            n = index * (EXPERTS - 1) + k - 1
            span = pl.ds(k * MAIN, MAIN)
            arriving["tok", index, k] = send(
                packs.at[index, span, :], tok.at[index, span, :],
                t_send.at[n], t_recv.at[n], place(s, at_x(k), z),
            )

    def normed(ref, pick):
        scale = scale_of(ref)
        return lambda c: nn(pick, (part(ref, c).astype(F32) * scale * part(gain_ref, c)).astype(BF16))

    pick_f, weight_f = layout(rf_ref, pf_ref)
    distribute(0, normed(x_ref, pick_f))
    pick_b, weight_b = layout(rb_ref, pb_ref)
    distribute(1, normed(act_ref, pick_b))
    high, low = two(weight_b)
    distribute(2, lambda c: nn(high, part(g_ref, c)) + nn(low, part(g_ref, c)))
    wf[...] = weight_f
    wb[...] = pick_b.astype(F32)
    arriving["x"] = send(x_ref, x_in, s_send.at[0], s_recv.at[0], ahead)
    arriving["wf"] = send(wf, wf_in, s_send.at[4], s_recv.at[4], ahead)
    arriving["act"] = send(act_ref, act_in, s_send.at[1], s_recv.at[1], behind)
    arriving["g"] = send(g_ref, g_in, s_send.at[2], s_recv.at[2], behind)
    arriving["gain"] = send(gain_ref, gain_in, s_send.at[3], s_recv.at[3], behind)
    arriving["wb"] = send(wb, wb_in, s_send.at[5], s_recv.at[5], behind)
    for copy in keep:
        copy.wait()

    def tokens_of(index):
        for k in range(1, EXPERTS):
            arriving["tok", index, k].wait_recv()
        for c, (at, size) in enumerate(parts):
            tail = width + c * LANE
            rest[index, :, at:at + size] = unfold(tok[index, :, tail:tail + LANE], size)

    def rows_of(index, c, which=parts):
        at, size = which[c]
        return [tok[index, :, at:at + size]], [rest[index, :, at:at + size]]

    def both_up(pair, c):
        one, other = (0, reach_a) if pair == 0 else (pair, reach_a + pair)
        at, size = parts[c]
        return jnp.concatenate([up[one, at:at + size, :], up[other, at:at + size, :]], axis=1)

    def both_down(pair, c):
        one, other = (0, reach_a) if pair == 0 else (pair, reach_a + pair)
        at, size = fine[c]
        return jnp.concatenate([down[one, :, at:at + size], down[other, :, at:at + size]], axis=0)

    def up_piece(c, pair):
        main_f, rest_f = rows_of(0, c)
        main_b, rest_b = rows_of(1, c)
        term = nn(jnp.concatenate(main_f + rest_f + main_b + rest_b, axis=0), both_up(pair, c))
        if c == 0:
            pre[pair] = term
        else:
            pre[pair] += term
        if c == pieces - 1:
            v = pre[pair, :SLOTS, :]
            hid[pair] = (v * jax.nn.sigmoid(v)).astype(BF16)

    def give_back(name, c, size, rows, src, dst, send_sem, recv_sem, section):
        src[c, :, :size] = rows[:MAINS]
        src[c, :, size:size + LANE] = fold(rows[MAINS:], size)
        for k in range(EXPERTS):
            span, lanes = pl.ds(k * MAIN, MAIN), pl.ds(0, size + LANE)
            arriving[name, c, k] = send(
                src.at[c, span, lanes], dst.at[c, span, lanes],
                send_sem.at[c, k], recv_sem.at[c, k], place(section, at_x(-k), z),
            )

    def down_back(c, pair):
        main_g, rest_g = rows_of(2, c, fine)
        term = nt(jnp.concatenate(main_g + rest_g, axis=0), both_down(pair, c))
        if c == 0:
            dh[pair] = term
        else:
            dh[pair] += term
        if c == fines - 1:
            v = pre[pair, SLOTS:, :]
            sig = jax.nn.sigmoid(v)
            dpre[pair] = (dh[pair] * sig * (1.0 + v * (1.0 - sig))).astype(BF16)

    def down_forward(c, pair):
        at, size = fine[c]
        term = nn(hid[pair], both_down(pair, c))
        if pair == 1 % pairs:
            out_acc[:, at:at + size] = term
        elif pair != 0:
            out_acc[:, at:at + size] += term
        else:
            rows = (out_acc[:, at:at + size] + term).astype(BF16)
            give_back("f", c, size, rows, ret_f, back_f, f_send, f_recv, nxt)

    def back_term(c, pair):
        at, size = parts[c]
        term = nt(dpre[pair], both_up(pair, c))
        if pair == 1 % pairs:
            dn_acc[:, at:at + size] = term
        else:
            dn_acc[:, at:at + size] += term

    waiting = []
    have_n = have_g = False
    for t in range(1, last + reach_a):
        if 3 <= t + 1 < last:
            start_own(t + 1)
        for r in range(1, reach_a + 1):
            c = t - r
            if 0 <= c < last:
                pass_round(c, r)
                waiting.append((c, r % reach_a))
        if t >= TOKEN_STEP:
            if not have_n:
                tokens_of(0)
                tokens_of(1)
                have_n = True
            for c, pair in waiting:
                if c < pieces:
                    up_piece(c, pair)
                    continue
                c = c - pieces
                if not have_g:
                    tokens_of(2)
                    have_g = True
                down_back(c, pair)
                if c < fines - 1 or pair != 0:
                    down_forward(c, pair)
                if c == fines - 1 and pair != 0:
                    for i in range(pieces):
                        back_term(i, pair)
            waiting = []

    order = [pieces - 1] + list(range(pieces - 1))
    for n, c in enumerate(order):
        at, size = parts[c]
        back_term(c, 0)
        give_back("b", c, size, dn_acc[:, at:at + size].astype(BF16), ret_b, back_b, b_send, b_recv, prv)
        if n == 0:
            down_forward(fines - 1, 0)

    for c, (at, size) in enumerate(parts):
        main_b, rest_b = rows_of(1, c)
        rows = jnp.concatenate(main_b + rest_b, axis=0).astype(F32)
        total = jnp.sum(rows * dn_acc[:, at:at + size], axis=0, keepdims=True)
        gpart[:, at:at + size] = total / part(gain_ref, c)
    gz[z] = gpart[...]
    for k in range(1, nz):
        send(gpart, gz.at[z], gz_send.at[k - 1], gz_recv.at[z], place(s, x, at_z(k)))

    def from_message(back, c, size):
        return jnp.concatenate([back[c, :, :size], unfold(back[c, :, size:size + LANE], size)], axis=0)

    for name in ("x", "wf", "act", "g", "gain", "wb"):
        arriving[name].wait_recv()
    scale = scale_of(act_in)
    high, low = two(wf_in[...])
    for c, (at, size) in enumerate(fine[:-1]):
        for k in range(EXPERTS):
            arriving["f", c, k].wait_recv()
        rows = from_message(back_f, c, size)
        act_out[:, at:at + size] = (x_in[:, at:at + size].astype(F32) + tn(high, rows) + tn(low, rows)).astype(BF16)

    for k in range(1, nz):
        frm = at_z(k)
        pltpu.make_async_remote_copy(
            src_ref=gpart, dst_ref=gz.at[frm], send_sem=gz_send.at[k - 1],
            recv_sem=gz_recv.at[frm], device_id=long_way, device_id_type=MESH,
        ).wait_recv()
    total = gz[0]
    for k in range(1, nz):
        total = total + gz[k]
    gx_own[...] = total
    gx[x] = total
    for k in range(1, EXPERTS):
        send(gx_own, gx.at[x], gx_send.at[k - 1], gx_recv.at[x], place(s, at_x(k), z))

    for c, (at, size) in list(enumerate(fine))[-1:]:
        for k in range(EXPERTS):
            arriving["f", c, k].wait_recv()
        rows = from_message(back_f, c, size)
        act_out[:, at:at + size] = (x_in[:, at:at + size].astype(F32) + tn(high, rows) + tn(low, rows)).astype(BF16)

    pick = wb_in[...].astype(BF16)
    dot = jnp.zeros((tokens, 1), F32)
    for c in order:
        at, size = parts[c]
        for k in range(EXPERTS):
            arriving["b", c, k].wait_recv()
        scaled = tn(pick, from_message(back_b, c, size)) * part(gain_in, c)
        qg[:, at:at + size] = scaled
        dot = dot + jnp.sum(scaled * (part(act_in, c).astype(F32) * scale), axis=-1, keepdims=True)
    mean = dot / width
    for c, (at, size) in enumerate(parts):
        xhat = part(act_in, c).astype(F32) * scale
        dx = part(g_in, c).astype(F32) + scale * (qg[:, at:at + size] - xhat * mean)
        grad_out[:, at:at + size] = dx.astype(BF16)

    for k in range(1, EXPERTS):
        frm = at_x(k)
        pltpu.make_async_remote_copy(
            src_ref=gx_own, dst_ref=gx.at[frm], send_sem=gx_send.at[k - 1],
            recv_sem=gx_recv.at[frm], device_id=long_way, device_id_type=MESH,
        ).wait_recv()
    total = gx[0]
    for k in range(1, EXPERTS):
        total = total + gx[k]
    gain_out[...] = total
    for copy in sent:
        copy.wait_send()


def body(sections, ranks, dp, x_fwd, gain, w_up, w_down, routes_f, probs_f, act_b, grad_b, routes_b, probs_b):
    zlo = ranks // EXPERTS
    nz = zlo * dp
    tokens, width = x_fwd.shape[1:]
    hidden = w_up.shape[-1]
    pairs = nz // 2
    pieces, fines = len(cuts(width)), len(cuts(width, FINE))
    last = pieces + fines
    span = width + pieces * LANE
    vmem, hbm = pl.BlockSpec(memory_space=pltpu.VMEM), pl.BlockSpec(memory_space=pl.ANY)
    dma = pltpu.SemaphoreType.DMA

    def bf16(*shape):
        return pltpu.VMEM(shape, BF16)

    def f32(*shape):
        return pltpu.VMEM(shape, F32)

    top = routes_f.shape[-1]
    routes = pltpu.VMEM((top, tokens), jnp.int32)
    scratch = [
        bf16(tokens, width), f32(1, width), routes, f32(top, tokens),
        bf16(tokens, width), bf16(tokens, width), routes, f32(top, tokens),
        bf16(nz, width, hidden), bf16(nz, hidden, width),
        bf16(3, MAINS, span), bf16(3, MAINS, span), bf16(3, SLOTS - MAINS, width),
        f32(pairs, 2 * SLOTS, 2 * hidden), bf16(pairs, SLOTS, 2 * hidden),
        f32(pairs, SLOTS, 2 * hidden), bf16(pairs, SLOTS, 2 * hidden),
        f32(SLOTS, width), f32(SLOTS, width),
    ]
    to_f, to_b = bf16(fines, MAINS, FINE + LANE), bf16(pieces, MAINS, PIECE + LANE)
    scratch += [to_f, to_b, to_f, to_b]
    scratch += [bf16(tokens, width)] * 3 + [f32(1, width)]
    scratch += [f32(SLOTS, tokens)] * 4 + [f32(tokens, width)]
    scratch += [f32(1, width), f32(nz, 1, width), f32(1, width), f32(EXPERTS, 1, width)]
    scratch += [
        dma((8,)), dma((2,)), dma((last, nz - 1)), dma((last, nz - 1)),
        dma((3 * (EXPERTS - 1),)), dma((3 * (EXPERTS - 1),)),
        dma((fines, EXPERTS)), dma((fines, EXPERTS)), dma((pieces, EXPERTS)), dma((pieces, EXPERTS)),
        dma((6,)), dma((6,)),
        dma((EXPERTS - 1,)), dma((EXPERTS,)), dma((nz - 1,)), dma((nz,)),
    ]
    act, grad, gain_grad = pl.pallas_call(
        functools.partial(relay, (sections, nz, zlo)),
        out_shape=(
            jax.ShapeDtypeStruct((tokens, width), BF16),
            jax.ShapeDtypeStruct((tokens, width), BF16),
            jax.ShapeDtypeStruct((1, width), F32),
        ),
        in_specs=[hbm] * 10,
        out_specs=(vmem, vmem, vmem),
        scratch_shapes=scratch,
        compiler_params=pltpu.CompilerParams(
            collective_id=0, has_side_effects=True, vmem_limit_bytes=56 * 2**20
        ),
    )(
        x_fwd[0], gain, w_up[0], w_down[0], routes_f[0].T, probs_f[0].T,
        act_b[0], grad_b[0], routes_b[0].T, probs_b[0].T,
    )
    return act[None], grad[None], gain_grad


def solution(mesh):
    sizes = mesh.shape
    rows, weights = P("section", ("expert", "dp"), None), P("section", None, ("expert", "dp"))
    return jax.shard_map(
        functools.partial(body, sizes["section"], sizes["expert"], sizes["dp"]),
        mesh=mesh,
        in_specs=(rows, P("section", None), weights) + (rows,) * 7,
        out_specs=(rows, rows, P("section", None)),
        check_vma=False,
    )
```

```python
import functools

import jax
import jax.numpy as jnp
from jax import lax
from jax.experimental import pallas as pl
from jax.experimental.pallas import tpu as pltpu
from jax.sharding import PartitionSpec as P

EXPERTS = 4
EPS = 1e-06
MAIN = 32
REST = 4
SLOTS = EXPERTS * (MAIN + REST)
MAINS = EXPERTS * MAIN
LANE = 128
PIECE = LANE * MAIN // REST
FINE = PIECE // 4
TOKEN_STEP = 4
FARTHEST = (2, 1, 3, 0)
MESH = pl.DeviceIdType.MESH
F32 = jnp.float32
BF16 = jnp.bfloat16


def nt(a, b):
    return lax.dot_general(a, b, (((1,), (1,)), ((), ())), preferred_element_type=F32)


def tn(a, b):
    return lax.dot_general(a, b, (((0,), (0,)), ((), ())), preferred_element_type=F32)


def nn(a, b):
    return jnp.dot(a, b, preferred_element_type=F32)


def cuts(width):
    return [(at, min(PIECE, width - at)) for at in range(0, width, PIECE)]


def fine_cuts(width):
    found, at = [], 0
    while at < width:
        size = min(PIECE, width - at, max(FINE, (width - at) // 2 // FINE * FINE))
        found.append((at, size))
        at += size
    return found


def relay(
    dims,
    x_hbm, gain_hbm, up_in, down_in, rf_hbm, pf_hbm, act_hbm, g_hbm, rb_hbm, pb_hbm,
    act_out, grad_out, gain_out,
    x_ref, gain_ref, rf_ref, pf_ref, act_ref, g_ref, rb_ref, pb_ref,
    up, down, packs, tok, rest, pre, hid, dh, dpre, out_acc, dn_acc, ret_f, ret_b, back_f, back_b,
    x_in, act_in, g_in, gain_in, wf, wb, wf_in, wb_in, qg, gpart, gz, gx_own, gx,
    in_sem, own_sem, z_send, z_recv, t_send, t_recv, f_send, f_recv, b_send, b_recv,
    s_send, s_recv, gx_send, gx_recv, gz_send, gz_recv,
):
    sections, nz, zlo = dims
    tokens, width = x_ref.shape
    parts = cuts(width)
    pieces = len(parts)
    fine = fine_cuts(width)
    fines = len(fine)
    all_cuts = parts + fine
    last = len(all_cuts)
    pairs = nz // 2
    s, e, d = lax.axis_index("section"), lax.axis_index("expert"), lax.axis_index("dp")
    x, z = e // zlo, d * zlo + e % zlo
    nxt, prv = lax.rem(s + 1, sections), lax.rem(s + sections - 1, sections)
    sign = 1 - 2 * lax.rem(s, 2)
    reach_a, reach_b = nz // 2, nz // 2 - 1

    def place(section, xx, zz):
        return (section, xx * zlo + lax.rem(zz, zlo), zz // zlo)

    def at_x(k):
        return lax.rem(x + k + EXPERTS, EXPERTS)

    def at_z(k):
        return lax.rem(z + k + nz, nz)

    peers = [place(s, x, at_z(k)) for k in range(1, nz)]
    peers += [place(s, at_x(k), z) for k in range(1, EXPERTS)]
    peers += [place(nxt, at_x(k), z) for k in range(EXPERTS)]
    peers += [place(prv, at_x(k), z) for k in range(EXPERTS)]
    barrier = pltpu.get_barrier_semaphore()
    for peer in peers:
        pl.semaphore_signal(barrier, inc=1, device_id=peer, device_id_type=MESH)
    fetched = [
        (rf_hbm, rf_ref), (rb_hbm, rb_ref), (pf_hbm, pf_ref), (pb_hbm, pb_ref), (gain_hbm, gain_ref),
        (x_hbm, x_ref), (act_hbm, act_ref), (g_hbm, g_ref),
    ]
    fetched = [pltpu.make_async_copy(a, b, in_sem.at[i]) for i, (a, b) in enumerate(fetched)]
    for copy in fetched:
        copy.start()
    pl.semaphore_wait(barrier, len(peers))

    sent = []

    def send(src, dst, send_sem, recv_sem, device):
        copy = pltpu.make_async_remote_copy(
            src_ref=src, dst_ref=dst, send_sem=send_sem, recv_sem=recv_sem,
            device_id=device, device_id_type=MESH,
        )
        copy.start()
        sent.append(copy)
        return copy

    long_way, short_way = place(s, x, at_z(sign)), place(s, x, at_z(-sign))
    moving = {}

    def own_piece(c):
        at, size = all_cuts[c]
        return up_in.at[pl.ds(at, size), :] if c < pieces else down_in.at[:, pl.ds(at, size)]

    def held(slot, c):
        at, size = all_cuts[c]
        return up.at[slot, pl.ds(at, size), :] if c < pieces else down.at[slot, :, pl.ds(at, size)]

    def pass_on(c, frm, to, device):
        src = own_piece(c) if frm == 0 else held(frm, c)
        moving[c, to] = send(
            src, held(to, c), z_send.at[c, to - 1], z_recv.at[c, to - 1], device
        )

    def start_own(c):
        pass_on(c, 0, 1, long_way)
        pass_on(c, 0, reach_a + 1, short_way)

    def pass_round(c, r):
        moving[c, r].wait_recv()
        if r < reach_a:
            pass_on(c, r, r + 1, long_way)
        if r <= reach_b:
            moving[c, reach_a + r].wait_recv()
            if r < reach_b:
                pass_on(c, reach_a + r, reach_a + r + 1, short_way)

    for c in range(3):
        start_own(c)
    keep = [pltpu.make_async_copy(up_in, up.at[0], own_sem.at[0]), pltpu.make_async_copy(down_in, down.at[0], own_sem.at[1])]
    for copy in keep:
        copy.start()
    for copy in fetched:
        copy.wait()

    ahead, behind = place(nxt, x, z), place(prv, x, z)
    arriving = {}

    row = lax.broadcasted_iota(jnp.int32, (SLOTS, tokens), 0)
    main = row < MAINS
    block = jnp.where(main, row // MAIN, (row - MAINS) // REST)
    slot = jnp.where(main, row % MAIN, MAIN + (row - MAINS) % REST).astype(F32)
    expert = x + block
    expert = jnp.where(expert >= EXPERTS, expert - EXPERTS, expert)
    earlier = (
        lax.broadcasted_iota(jnp.int32, (tokens, tokens), 0)
        < lax.broadcasted_iota(jnp.int32, (tokens, tokens), 1)
    ).astype(F32).astype(BF16)

    def layout(r_ref, p_ref):
        first, second = r_ref[0:1, :] == expert, r_ref[1:2, :] == expert
        chosen = jnp.where(first | second, 1.0, 0.0)
        before = nn(chosen.astype(BF16), earlier)
        taken = (before == slot) & (chosen > 0.5)
        weight = jnp.where(first, p_ref[0:1, :], 0.0) + jnp.where(second, p_ref[1:2, :], 0.0)
        return jnp.where(taken, 1.0, 0.0).astype(BF16), jnp.where(taken, weight, 0.0)

    def two(w):
        high = w.astype(BF16)
        return high, (w - high.astype(F32)).astype(BF16)

    def rest_out(tiles):
        a = lax.broadcasted_iota(jnp.int32, (MAINS, tiles * EXPERTS * REST), 0)
        b = lax.broadcasted_iota(jnp.int32, (MAINS, tiles * EXPERTS * REST), 1)
        source = (a % MAIN // REST) * (EXPERTS * REST) + (a // MAIN) * REST + a % REST
        return jnp.where(source == b, 1.0, 0.0).astype(BF16)

    moves = {size // LANE: rest_out(size // LANE) for _, size in all_cuts}

    def fold(rows, size):
        tiles = size // LANE
        stack = jnp.concatenate([rows[:, i * LANE:(i + 1) * LANE] for i in range(tiles)], axis=0)
        return nn(moves[tiles], stack).astype(BF16)

    def unfold(message, size):
        tiles, deep = size // LANE, EXPERTS * REST
        stack = tn(moves[tiles], message).astype(BF16)
        return jnp.concatenate([stack[i * deep:(i + 1) * deep] for i in range(tiles)], axis=1)

    def part(ref, c):
        at, size = parts[c]
        return ref[:, at:at + size]

    def scale_of(ref):
        total = jnp.zeros((tokens, 1), F32)
        for c in range(pieces):
            v = part(ref, c).astype(F32)
            total = total + jnp.sum(v * v, axis=-1, keepdims=True)
        return lax.rsqrt(total / width + EPS)

    def distribute(index, rows_of):
        for c, (at, size) in enumerate(parts):
            rows = rows_of(c).astype(BF16)
            low = fold(rows[MAINS:], size)
            tail = width + c * LANE
            packs[index, :, at:at + size] = rows[:MAINS]
            packs[index, :, tail:tail + LANE] = low
            tok[index, :MAIN, at:at + size] = rows[:MAIN]
            tok[index, :MAIN, tail:tail + LANE] = low[:MAIN]
        for k in FARTHEST[:-1]:
            n = index * (EXPERTS - 1) + k - 1
            span = pl.ds(k * MAIN, MAIN)
            arriving["tok", index, k] = send(
                packs.at[index, span, :], tok.at[index, span, :],
                t_send.at[n], t_recv.at[n], place(s, at_x(k), z),
            )

    def normed(ref, pick):
        scale = scale_of(ref)
        return lambda c: nn(pick, (part(ref, c).astype(F32) * scale * part(gain_ref, c)).astype(BF16))

    pick_f, weight_f = layout(rf_ref, pf_ref)
    distribute(0, normed(x_ref, pick_f))
    pick_b, weight_b = layout(rb_ref, pb_ref)
    distribute(1, normed(act_ref, pick_b))
    high, low = two(weight_b)
    distribute(2, lambda c: nn(high, part(g_ref, c)) + nn(low, part(g_ref, c)))
    wf[...] = weight_f
    wb[...] = pick_b.astype(F32)
    arriving["x"] = send(x_ref, x_in, s_send.at[0], s_recv.at[0], ahead)
    arriving["wf"] = send(wf, wf_in, s_send.at[4], s_recv.at[4], ahead)
    arriving["act"] = send(act_ref, act_in, s_send.at[1], s_recv.at[1], behind)
    arriving["g"] = send(g_ref, g_in, s_send.at[2], s_recv.at[2], behind)
    arriving["gain"] = send(gain_ref, gain_in, s_send.at[3], s_recv.at[3], behind)
    arriving["wb"] = send(wb, wb_in, s_send.at[5], s_recv.at[5], behind)
    for copy in keep:
        copy.wait()

    def tokens_of(index):
        for k in range(1, EXPERTS):
            arriving["tok", index, k].wait_recv()
        for c, (at, size) in enumerate(parts):
            tail = width + c * LANE
            rest[index, :, at:at + size] = unfold(tok[index, :, tail:tail + LANE], size)

    def rows_of(index, c, which=parts):
        at, size = which[c]
        return [tok[index, :, at:at + size]], [rest[index, :, at:at + size]]

    def both_up(pair, c):
        one, other = (0, reach_a) if pair == 0 else (pair, reach_a + pair)
        at, size = parts[c]
        return jnp.concatenate([up[one, at:at + size, :], up[other, at:at + size, :]], axis=1)

    def both_down(pair, c):
        one, other = (0, reach_a) if pair == 0 else (pair, reach_a + pair)
        at, size = fine[c]
        return jnp.concatenate([down[one, :, at:at + size], down[other, :, at:at + size]], axis=0)

    def up_piece(c, pair):
        main_f, rest_f = rows_of(0, c)
        main_b, rest_b = rows_of(1, c)
        term = nn(jnp.concatenate(main_f + rest_f + main_b + rest_b, axis=0), both_up(pair, c))
        if c == 0:
            pre[pair] = term
        else:
            pre[pair] += term
        if c == pieces - 1:
            v = pre[pair, :SLOTS, :]
            hid[pair] = (v * jax.nn.sigmoid(v)).astype(BF16)

    def give_back(name, c, size, rows, src, dst, send_sem, recv_sem, section):
        src[c, :, :size] = rows[:MAINS]
        src[c, :, size:size + LANE] = fold(rows[MAINS:], size)
        for k in FARTHEST:
            span, lanes = pl.ds(k * MAIN, MAIN), pl.ds(0, size + LANE)
            arriving[name, c, k] = send(
                src.at[c, span, lanes], dst.at[c, span, lanes],
                send_sem.at[c, k], recv_sem.at[c, k], place(section, at_x(-k), z),
            )

    def down_back(c, pair):
        main_g, rest_g = rows_of(2, c, fine)
        term = nt(jnp.concatenate(main_g + rest_g, axis=0), both_down(pair, c))
        if c == 0:
            dh[pair] = term
        else:
            dh[pair] += term
        if c == fines - 1:
            v = pre[pair, SLOTS:, :]
            sig = jax.nn.sigmoid(v)
            dpre[pair] = (dh[pair] * sig * (1.0 + v * (1.0 - sig))).astype(BF16)

    def down_forward(c, pair):
        at, size = fine[c]
        term = nn(hid[pair], both_down(pair, c))
        if pair == 1 % pairs:
            out_acc[:, at:at + size] = term
        elif pair != 0:
            out_acc[:, at:at + size] += term
        else:
            rows = (out_acc[:, at:at + size] + term).astype(BF16)
            give_back("f", c, size, rows, ret_f, back_f, f_send, f_recv, nxt)

    def back_term(c, pair):
        at, size = parts[c]
        term = nt(dpre[pair], both_up(pair, c))
        if pair == 1 % pairs:
            dn_acc[:, at:at + size] = term
        else:
            dn_acc[:, at:at + size] += term

    waiting = []
    have_n = have_g = False
    for t in range(1, last + reach_a):
        if 3 <= t + 1 < last:
            start_own(t + 1)
        for r in range(1, reach_a + 1):
            c = t - r
            if 0 <= c < last:
                pass_round(c, r)
                waiting.append((c, r % reach_a))
        if t >= TOKEN_STEP:
            if not have_n:
                tokens_of(0)
                tokens_of(1)
                have_n = True
            for c, pair in waiting:
                if c < pieces:
                    up_piece(c, pair)
                    continue
                c = c - pieces
                if not have_g:
                    tokens_of(2)
                    have_g = True
                down_back(c, pair)
                if c < fines - 1 or pair != 0:
                    down_forward(c, pair)
                if c == fines - 1 and pair != 0:
                    for i in range(pieces):
                        back_term(i, pair)
            waiting = []

    order = [pieces - 1] + list(range(pieces - 1))
    for c in order:
        at, size = parts[c]
        back_term(c, 0)
        give_back("b", c, size, dn_acc[:, at:at + size].astype(BF16), ret_b, back_b, b_send, b_recv, prv)
    down_forward(fines - 1, 0)

    for c, (at, size) in enumerate(parts):
        main_b, rest_b = rows_of(1, c)
        rows = jnp.concatenate(main_b + rest_b, axis=0).astype(F32)
        total = jnp.sum(rows * dn_acc[:, at:at + size], axis=0, keepdims=True)
        gpart[:, at:at + size] = total / part(gain_ref, c)
    gz[z] = gpart[...]
    for k in range(1, nz):
        send(gpart, gz.at[z], gz_send.at[k - 1], gz_recv.at[z], place(s, x, at_z(k)))

    def from_message(back, c, size):
        return jnp.concatenate([back[c, :, :size], unfold(back[c, :, size:size + LANE], size)], axis=0)

    for name in ("x", "wf", "act", "g", "gain", "wb"):
        arriving[name].wait_recv()
    scale = scale_of(act_in)
    high, low = two(wf_in[...])
    for c, (at, size) in enumerate(fine[:-1]):
        for k in range(EXPERTS):
            arriving["f", c, k].wait_recv()
        rows = from_message(back_f, c, size)
        act_out[:, at:at + size] = (x_in[:, at:at + size].astype(F32) + tn(high, rows) + tn(low, rows)).astype(BF16)

    for k in range(1, nz):
        frm = at_z(k)
        pltpu.make_async_remote_copy(
            src_ref=gpart, dst_ref=gz.at[frm], send_sem=gz_send.at[k - 1],
            recv_sem=gz_recv.at[frm], device_id=long_way, device_id_type=MESH,
        ).wait_recv()
    total = gz[0]
    for k in range(1, nz):
        total = total + gz[k]
    gx_own[...] = total
    gx[x] = total
    for k in range(1, EXPERTS):
        send(gx_own, gx.at[x], gx_send.at[k - 1], gx_recv.at[x], place(s, at_x(k), z))

    pick = wb_in[...].astype(BF16)
    dot = jnp.zeros((tokens, 1), F32)
    for c in order:
        at, size = parts[c]
        for k in range(EXPERTS):
            arriving["b", c, k].wait_recv()
        scaled = tn(pick, from_message(back_b, c, size)) * part(gain_in, c)
        qg[:, at:at + size] = scaled
        dot = dot + jnp.sum(scaled * (part(act_in, c).astype(F32) * scale), axis=-1, keepdims=True)
    mean = dot / width
    for c, (at, size) in enumerate(parts):
        xhat = part(act_in, c).astype(F32) * scale
        dx = part(g_in, c).astype(F32) + scale * (qg[:, at:at + size] - xhat * mean)
        grad_out[:, at:at + size] = dx.astype(BF16)

    for c, (at, size) in list(enumerate(fine))[-1:]:
        for k in range(EXPERTS):
            arriving["f", c, k].wait_recv()
        rows = from_message(back_f, c, size)
        act_out[:, at:at + size] = (x_in[:, at:at + size].astype(F32) + tn(high, rows) + tn(low, rows)).astype(BF16)

    for k in range(1, EXPERTS):
        frm = at_x(k)
        pltpu.make_async_remote_copy(
            src_ref=gx_own, dst_ref=gx.at[frm], send_sem=gx_send.at[k - 1],
            recv_sem=gx_recv.at[frm], device_id=long_way, device_id_type=MESH,
        ).wait_recv()
    total = gx[0]
    for k in range(1, EXPERTS):
        total = total + gx[k]
    gain_out[...] = total
    for copy in sent:
        copy.wait_send()


def body(sections, ranks, dp, x_fwd, gain, w_up, w_down, routes_f, probs_f, act_b, grad_b, routes_b, probs_b):
    zlo = ranks // EXPERTS
    nz = zlo * dp
    tokens, width = x_fwd.shape[1:]
    hidden = w_up.shape[-1]
    pairs = nz // 2
    pieces, fines = len(cuts(width)), len(fine_cuts(width))
    last = pieces + fines
    span = width + pieces * LANE
    vmem, hbm = pl.BlockSpec(memory_space=pltpu.VMEM), pl.BlockSpec(memory_space=pl.ANY)
    dma = pltpu.SemaphoreType.DMA

    def bf16(*shape):
        return pltpu.VMEM(shape, BF16)

    def f32(*shape):
        return pltpu.VMEM(shape, F32)

    top = routes_f.shape[-1]
    routes = pltpu.VMEM((top, tokens), jnp.int32)
    scratch = [
        bf16(tokens, width), f32(1, width), routes, f32(top, tokens),
        bf16(tokens, width), bf16(tokens, width), routes, f32(top, tokens),
        bf16(nz, width, hidden), bf16(nz, hidden, width),
        bf16(3, MAINS, span), bf16(3, MAINS, span), bf16(3, SLOTS - MAINS, width),
        f32(pairs, 2 * SLOTS, 2 * hidden), bf16(pairs, SLOTS, 2 * hidden),
        f32(pairs, SLOTS, 2 * hidden), bf16(pairs, SLOTS, 2 * hidden),
        f32(SLOTS, width), f32(SLOTS, width),
    ]
    to_f, to_b = bf16(fines, MAINS, PIECE + LANE), bf16(pieces, MAINS, PIECE + LANE)
    scratch += [to_f, to_b, to_f, to_b]
    scratch += [bf16(tokens, width)] * 3 + [f32(1, width)]
    scratch += [f32(SLOTS, tokens)] * 4 + [f32(tokens, width)]
    scratch += [f32(1, width), f32(nz, 1, width), f32(1, width), f32(EXPERTS, 1, width)]
    scratch += [
        dma((8,)), dma((2,)), dma((last, nz - 1)), dma((last, nz - 1)),
        dma((3 * (EXPERTS - 1),)), dma((3 * (EXPERTS - 1),)),
        dma((fines, EXPERTS)), dma((fines, EXPERTS)), dma((pieces, EXPERTS)), dma((pieces, EXPERTS)),
        dma((6,)), dma((6,)),
        dma((EXPERTS - 1,)), dma((EXPERTS,)), dma((nz - 1,)), dma((nz,)),
    ]
    act, grad, gain_grad = pl.pallas_call(
        functools.partial(relay, (sections, nz, zlo)),
        out_shape=(
            jax.ShapeDtypeStruct((tokens, width), BF16),
            jax.ShapeDtypeStruct((tokens, width), BF16),
            jax.ShapeDtypeStruct((1, width), F32),
        ),
        in_specs=[hbm] * 10,
        out_specs=(vmem, vmem, vmem),
        scratch_shapes=scratch,
        compiler_params=pltpu.CompilerParams(
            collective_id=0, has_side_effects=True, vmem_limit_bytes=56 * 2**20
        ),
    )(
        x_fwd[0], gain, w_up[0], w_down[0], routes_f[0].T, probs_f[0].T,
        act_b[0], grad_b[0], routes_b[0].T, probs_b[0].T,
    )
    return act[None], grad[None], gain_grad


def solution(mesh):
    sizes = mesh.shape
    rows, weights = P("section", ("expert", "dp"), None), P("section", None, ("expert", "dp"))
    return jax.shard_map(
        functools.partial(body, sizes["section"], sizes["expert"], sizes["dp"]),
        mesh=mesh,
        in_specs=(rows, P("section", None), weights) + (rows,) * 7,
        out_specs=(rows, rows, P("section", None)),
        check_vma=False,
    )
```

```python
import functools

import jax
import jax.numpy as jnp
from jax import lax
from jax.experimental import pallas as pl
from jax.experimental.pallas import tpu as pltpu
from jax.sharding import PartitionSpec as P

EXPERTS = 4
EPS = 1e-06
MAIN = 32
REST = 4
SLOTS = EXPERTS * (MAIN + REST)
MAINS = EXPERTS * MAIN
LANE = 128
PIECE = LANE * MAIN // REST
FINE = PIECE // 4
TOKEN_STEP = 4
FARTHEST = (2, 1, 3, 0)
MESH = pl.DeviceIdType.MESH
F32 = jnp.float32
BF16 = jnp.bfloat16


def nt(a, b):
    return lax.dot_general(a, b, (((1,), (1,)), ((), ())), preferred_element_type=F32)


def tn(a, b):
    return lax.dot_general(a, b, (((0,), (0,)), ((), ())), preferred_element_type=F32)


def nn(a, b):
    return jnp.dot(a, b, preferred_element_type=F32)


def cuts(width):
    return [(at, min(PIECE, width - at)) for at in range(0, width, PIECE)]


def fine_cuts(width):
    found, at = [], 0
    while at < width:
        size = min(PIECE, width - at, max(FINE, (width - at) // 2 // FINE * FINE))
        found.append((at, size))
        at += size
    return found


def relay(
    dims,
    x_hbm, gain_hbm, up_in, down_in, rf_hbm, pf_hbm, act_hbm, g_hbm, rb_hbm, pb_hbm,
    act_out, grad_out, gain_out,
    x_ref, gain_ref, rf_ref, pf_ref, act_ref, g_ref, rb_ref, pb_ref,
    up, down, packs, tok, rest, pre, hid, dh, dpre, out_acc, dn_acc, ret_f, ret_b, back_f, back_b,
    x_in, act_in, g_in, gain_in, wf, wb, wf_in, wb_in, qg, gpart, gz, gx_own, gx,
    in_sem, own_sem, z_send, z_recv, t_send, t_recv, f_send, f_recv, b_send, b_recv,
    s_send, s_recv, gx_send, gx_recv, gz_send, gz_recv,
):
    sections, nz, zlo = dims
    tokens, width = x_ref.shape
    parts = cuts(width)
    pieces = len(parts)
    fine = fine_cuts(width)
    fines = len(fine)
    all_cuts = parts + fine
    last = len(all_cuts)
    pairs = nz // 2
    s, e, d = lax.axis_index("section"), lax.axis_index("expert"), lax.axis_index("dp")
    x, z = e // zlo, d * zlo + e % zlo
    nxt, prv = lax.rem(s + 1, sections), lax.rem(s + sections - 1, sections)
    sign = 1 - 2 * lax.rem(s, 2)
    reach_a, reach_b = nz // 2, nz // 2 - 1

    def place(section, xx, zz):
        return (section, xx * zlo + lax.rem(zz, zlo), zz // zlo)

    def at_x(k):
        return lax.rem(x + k + EXPERTS, EXPERTS)

    def at_z(k):
        return lax.rem(z + k + nz, nz)

    peers = [place(s, x, at_z(k)) for k in range(1, nz)]
    peers += [place(s, at_x(k), z) for k in range(1, EXPERTS)]
    peers += [place(nxt, at_x(k), z) for k in range(EXPERTS)]
    peers += [place(prv, at_x(k), z) for k in range(EXPERTS)]
    barrier = pltpu.get_barrier_semaphore()
    for peer in peers:
        pl.semaphore_signal(barrier, inc=1, device_id=peer, device_id_type=MESH)
    fetched = [
        (rf_hbm, rf_ref), (rb_hbm, rb_ref), (pf_hbm, pf_ref), (pb_hbm, pb_ref), (gain_hbm, gain_ref),
        (x_hbm, x_ref), (act_hbm, act_ref), (g_hbm, g_ref),
    ]
    fetched = [pltpu.make_async_copy(a, b, in_sem.at[i]) for i, (a, b) in enumerate(fetched)]
    for copy in fetched:
        copy.start()
    pl.semaphore_wait(barrier, len(peers))

    sent = []

    def send(src, dst, send_sem, recv_sem, device):
        copy = pltpu.make_async_remote_copy(
            src_ref=src, dst_ref=dst, send_sem=send_sem, recv_sem=recv_sem,
            device_id=device, device_id_type=MESH,
        )
        copy.start()
        sent.append(copy)
        return copy

    long_way, short_way = place(s, x, at_z(sign)), place(s, x, at_z(-sign))
    moving = {}

    def own_piece(c):
        at, size = all_cuts[c]
        return up_in.at[pl.ds(at, size), :] if c < pieces else down_in.at[:, pl.ds(at, size)]

    def held(slot, c):
        at, size = all_cuts[c]
        return up.at[slot, pl.ds(at, size), :] if c < pieces else down.at[slot, :, pl.ds(at, size)]

    def pass_on(c, frm, to, device):
        src = own_piece(c) if frm == 0 else held(frm, c)
        moving[c, to] = send(
            src, held(to, c), z_send.at[c, to - 1], z_recv.at[c, to - 1], device
        )

    def start_own(c):
        pass_on(c, 0, 1, long_way)
        pass_on(c, 0, reach_a + 1, short_way)

    def pass_round(c, r):
        moving[c, r].wait_recv()
        if r < reach_a:
            pass_on(c, r, r + 1, long_way)
        if r <= reach_b:
            moving[c, reach_a + r].wait_recv()
            if r < reach_b:
                pass_on(c, reach_a + r, reach_a + r + 1, short_way)

    for c in range(3):
        start_own(c)
    keep = [pltpu.make_async_copy(up_in, up.at[0], own_sem.at[0]), pltpu.make_async_copy(down_in, down.at[0], own_sem.at[1])]
    for copy in keep:
        copy.start()
    for copy in fetched:
        copy.wait()

    ahead, behind = place(nxt, x, z), place(prv, x, z)
    arriving = {}

    row = lax.broadcasted_iota(jnp.int32, (SLOTS, tokens), 0)
    main = row < MAINS
    block = jnp.where(main, row // MAIN, (row - MAINS) // REST)
    slot = jnp.where(main, row % MAIN, MAIN + (row - MAINS) % REST).astype(F32)
    expert = x + block
    expert = jnp.where(expert >= EXPERTS, expert - EXPERTS, expert)
    earlier = (
        lax.broadcasted_iota(jnp.int32, (tokens, tokens), 0)
        < lax.broadcasted_iota(jnp.int32, (tokens, tokens), 1)
    ).astype(F32).astype(BF16)

    def layout(r_ref, p_ref):
        first, second = r_ref[0:1, :] == expert, r_ref[1:2, :] == expert
        chosen = jnp.where(first | second, 1.0, 0.0)
        before = nn(chosen.astype(BF16), earlier)
        taken = (before == slot) & (chosen > 0.5)
        weight = jnp.where(first, p_ref[0:1, :], 0.0) + jnp.where(second, p_ref[1:2, :], 0.0)
        return jnp.where(taken, 1.0, 0.0).astype(BF16), jnp.where(taken, weight, 0.0)

    def two(w):
        high = w.astype(BF16)
        return high, (w - high.astype(F32)).astype(BF16)

    def rest_out(tiles):
        a = lax.broadcasted_iota(jnp.int32, (MAINS, tiles * EXPERTS * REST), 0)
        b = lax.broadcasted_iota(jnp.int32, (MAINS, tiles * EXPERTS * REST), 1)
        source = (a % MAIN // REST) * (EXPERTS * REST) + (a // MAIN) * REST + a % REST
        return jnp.where(source == b, 1.0, 0.0).astype(BF16)

    moves = {size // LANE: rest_out(size // LANE) for _, size in all_cuts}

    def fold(rows, size):
        tiles = size // LANE
        stack = jnp.concatenate([rows[:, i * LANE:(i + 1) * LANE] for i in range(tiles)], axis=0)
        return nn(moves[tiles], stack).astype(BF16)

    def unfold(message, size):
        tiles, deep = size // LANE, EXPERTS * REST
        stack = tn(moves[tiles], message).astype(BF16)
        return jnp.concatenate([stack[i * deep:(i + 1) * deep] for i in range(tiles)], axis=1)

    def part(ref, c):
        at, size = parts[c]
        return ref[:, at:at + size]

    def scale_of(ref):
        total = jnp.zeros((tokens, 1), F32)
        for c in range(pieces):
            v = part(ref, c).astype(F32)
            total = total + jnp.sum(v * v, axis=-1, keepdims=True)
        return lax.rsqrt(total / width + EPS)

    def distribute(index, rows_of):
        for c, (at, size) in enumerate(parts):
            rows = rows_of(c).astype(BF16)
            low = fold(rows[MAINS:], size)
            tail = width + c * LANE
            packs[index, :, at:at + size] = rows[:MAINS]
            packs[index, :, tail:tail + LANE] = low
            tok[index, :MAIN, at:at + size] = rows[:MAIN]
            tok[index, :MAIN, tail:tail + LANE] = low[:MAIN]
        for k in FARTHEST[:-1]:
            n = index * (EXPERTS - 1) + k - 1
            span = pl.ds(k * MAIN, MAIN)
            arriving["tok", index, k] = send(
                packs.at[index, span, :], tok.at[index, span, :],
                t_send.at[n], t_recv.at[n], place(s, at_x(k), z),
            )

    def normed(ref, pick):
        scale = scale_of(ref)
        return lambda c: nn(pick, (part(ref, c).astype(F32) * scale * part(gain_ref, c)).astype(BF16))

    pick_f, weight_f = layout(rf_ref, pf_ref)
    distribute(0, normed(x_ref, pick_f))
    pick_b, weight_b = layout(rb_ref, pb_ref)
    distribute(1, normed(act_ref, pick_b))
    high, low = two(weight_b)
    distribute(2, lambda c: nn(high, part(g_ref, c)) + nn(low, part(g_ref, c)))
    wf[...] = weight_f
    wb[...] = pick_b.astype(F32)
    arriving["x"] = send(x_ref, x_in, s_send.at[0], s_recv.at[0], ahead)
    arriving["wf"] = send(wf, wf_in, s_send.at[4], s_recv.at[4], ahead)
    arriving["act"] = send(act_ref, act_in, s_send.at[1], s_recv.at[1], behind)
    arriving["g"] = send(g_ref, g_in, s_send.at[2], s_recv.at[2], behind)
    arriving["gain"] = send(gain_ref, gain_in, s_send.at[3], s_recv.at[3], behind)
    arriving["wb"] = send(wb, wb_in, s_send.at[5], s_recv.at[5], behind)
    for copy in keep:
        copy.wait()

    def tokens_of(index):
        for k in range(1, EXPERTS):
            arriving["tok", index, k].wait_recv()
        for c, (at, size) in enumerate(parts):
            tail = width + c * LANE
            rest[index, :, at:at + size] = unfold(tok[index, :, tail:tail + LANE], size)

    def rows_of(index, c, which=parts):
        at, size = which[c]
        return [tok[index, :, at:at + size]], [rest[index, :, at:at + size]]

    def both_up(pair, c):
        one, other = (0, reach_a) if pair == 0 else (pair, reach_a + pair)
        at, size = parts[c]
        return jnp.concatenate([up[one, at:at + size, :], up[other, at:at + size, :]], axis=1)

    def both_down(pair, c):
        one, other = (0, reach_a) if pair == 0 else (pair, reach_a + pair)
        at, size = fine[c]
        return jnp.concatenate([down[one, :, at:at + size], down[other, :, at:at + size]], axis=0)

    def up_piece(c, pair):
        main_f, rest_f = rows_of(0, c)
        main_b, rest_b = rows_of(1, c)
        term = nn(jnp.concatenate(main_f + rest_f + main_b + rest_b, axis=0), both_up(pair, c))
        if c == 0:
            pre[pair] = term
        else:
            pre[pair] += term
        if c == pieces - 1:
            v = pre[pair, :SLOTS, :]
            hid[pair] = (v * jax.nn.sigmoid(v)).astype(BF16)

    def give_back(name, c, size, rows, src, dst, send_sem, recv_sem, section):
        src[c, :, :size] = rows[:MAINS]
        src[c, :, size:size + LANE] = fold(rows[MAINS:], size)
        for k in FARTHEST:
            span, lanes = pl.ds(k * MAIN, MAIN), pl.ds(0, size + LANE)
            arriving[name, c, k] = send(
                src.at[c, span, lanes], dst.at[c, span, lanes],
                send_sem.at[c, k], recv_sem.at[c, k], place(section, at_x(-k), z),
            )

    def down_back(c, pair):
        main_g, rest_g = rows_of(2, c, fine)
        term = nt(jnp.concatenate(main_g + rest_g, axis=0), both_down(pair, c))
        if c == 0:
            dh[pair] = term
        else:
            dh[pair] += term
        if c == fines - 1:
            v = pre[pair, SLOTS:, :]
            sig = jax.nn.sigmoid(v)
            dpre[pair] = (dh[pair] * sig * (1.0 + v * (1.0 - sig))).astype(BF16)

    def down_forward(c, pair):
        at, size = fine[c]
        term = nn(hid[pair], both_down(pair, c))
        if pair == 1 % pairs:
            out_acc[:, at:at + size] = term
        elif pair != 0:
            out_acc[:, at:at + size] += term
        else:
            rows = (out_acc[:, at:at + size] + term).astype(BF16)
            give_back("f", c, size, rows, ret_f, back_f, f_send, f_recv, nxt)

    def back_term(c, pair):
        at, size = parts[c]
        term = nt(dpre[pair], both_up(pair, c))
        if pair == 1 % pairs:
            dn_acc[:, at:at + size] = term
        else:
            dn_acc[:, at:at + size] += term

    waiting, ready = [], []
    have_n = have_g = False
    for t in range(1, last + reach_a):
        if 3 <= t + 1 < last:
            start_own(t + 1)
        for r in range(1, reach_a + 1):
            c = t - r
            if 0 <= c < last:
                pass_round(c, r)
                waiting.append((c, r % reach_a))
        if t >= TOKEN_STEP:
            if not have_n:
                tokens_of(0)
                tokens_of(1)
                have_n = True
            for c, pair in waiting:
                if c < pieces:
                    up_piece(c, pair)
                    continue
                c = c - pieces
                if not have_g:
                    tokens_of(2)
                    have_g = True
                down_back(c, pair)
                if c < fines - 1 or pair != 0:
                    down_forward(c, pair)
                if c == fines - 1 and pair != 0:
                    ready.append(pair)
            waiting = []
            if t >= last + reach_a - 2:
                for pair in ready:
                    for i in range(pieces):
                        back_term(i, pair)
                ready = []

    order = [pieces - 1] + list(range(pieces - 1))
    for c in order:
        at, size = parts[c]
        back_term(c, 0)
        give_back("b", c, size, dn_acc[:, at:at + size].astype(BF16), ret_b, back_b, b_send, b_recv, prv)
    down_forward(fines - 1, 0)

    for c, (at, size) in enumerate(parts):
        main_b, rest_b = rows_of(1, c)
        rows = jnp.concatenate(main_b + rest_b, axis=0).astype(F32)
        total = jnp.sum(rows * dn_acc[:, at:at + size], axis=0, keepdims=True)
        gpart[:, at:at + size] = total / part(gain_ref, c)
    gz[z] = gpart[...]
    for k in range(1, nz):
        send(gpart, gz.at[z], gz_send.at[k - 1], gz_recv.at[z], place(s, x, at_z(k)))

    def from_message(back, c, size):
        return jnp.concatenate([back[c, :, :size], unfold(back[c, :, size:size + LANE], size)], axis=0)

    for name in ("x", "wf", "act", "g", "gain", "wb"):
        arriving[name].wait_recv()
    scale = scale_of(act_in)
    high, low = two(wf_in[...])
    for c, (at, size) in enumerate(fine[:-1]):
        for k in range(EXPERTS):
            arriving["f", c, k].wait_recv()
        rows = from_message(back_f, c, size)
        act_out[:, at:at + size] = (x_in[:, at:at + size].astype(F32) + tn(high, rows) + tn(low, rows)).astype(BF16)

    for k in range(1, nz):
        frm = at_z(k)
        pltpu.make_async_remote_copy(
            src_ref=gpart, dst_ref=gz.at[frm], send_sem=gz_send.at[k - 1],
            recv_sem=gz_recv.at[frm], device_id=long_way, device_id_type=MESH,
        ).wait_recv()
    total = gz[0]
    for k in range(1, nz):
        total = total + gz[k]
    gx_own[...] = total
    gx[x] = total
    for k in range(1, EXPERTS):
        send(gx_own, gx.at[x], gx_send.at[k - 1], gx_recv.at[x], place(s, at_x(k), z))

    pick = wb_in[...].astype(BF16)
    dot = jnp.zeros((tokens, 1), F32)
    for c in order:
        at, size = parts[c]
        for k in range(EXPERTS):
            arriving["b", c, k].wait_recv()
        scaled = tn(pick, from_message(back_b, c, size)) * part(gain_in, c)
        qg[:, at:at + size] = scaled
        dot = dot + jnp.sum(scaled * (part(act_in, c).astype(F32) * scale), axis=-1, keepdims=True)
    mean = dot / width
    for c, (at, size) in enumerate(parts):
        xhat = part(act_in, c).astype(F32) * scale
        dx = part(g_in, c).astype(F32) + scale * (qg[:, at:at + size] - xhat * mean)
        grad_out[:, at:at + size] = dx.astype(BF16)

    for c, (at, size) in list(enumerate(fine))[-1:]:
        for k in range(EXPERTS):
            arriving["f", c, k].wait_recv()
        rows = from_message(back_f, c, size)
        act_out[:, at:at + size] = (x_in[:, at:at + size].astype(F32) + tn(high, rows) + tn(low, rows)).astype(BF16)

    for k in range(1, EXPERTS):
        frm = at_x(k)
        pltpu.make_async_remote_copy(
            src_ref=gx_own, dst_ref=gx.at[frm], send_sem=gx_send.at[k - 1],
            recv_sem=gx_recv.at[frm], device_id=long_way, device_id_type=MESH,
        ).wait_recv()
    total = gx[0]
    for k in range(1, EXPERTS):
        total = total + gx[k]
    gain_out[...] = total
    for copy in sent:
        copy.wait_send()


def body(sections, ranks, dp, x_fwd, gain, w_up, w_down, routes_f, probs_f, act_b, grad_b, routes_b, probs_b):
    zlo = ranks // EXPERTS
    nz = zlo * dp
    tokens, width = x_fwd.shape[1:]
    hidden = w_up.shape[-1]
    pairs = nz // 2
    pieces, fines = len(cuts(width)), len(fine_cuts(width))
    last = pieces + fines
    span = width + pieces * LANE
    vmem, hbm = pl.BlockSpec(memory_space=pltpu.VMEM), pl.BlockSpec(memory_space=pl.ANY)
    dma = pltpu.SemaphoreType.DMA

    def bf16(*shape):
        return pltpu.VMEM(shape, BF16)

    def f32(*shape):
        return pltpu.VMEM(shape, F32)

    top = routes_f.shape[-1]
    routes = pltpu.VMEM((top, tokens), jnp.int32)
    scratch = [
        bf16(tokens, width), f32(1, width), routes, f32(top, tokens),
        bf16(tokens, width), bf16(tokens, width), routes, f32(top, tokens),
        bf16(nz, width, hidden), bf16(nz, hidden, width),
        bf16(3, MAINS, span), bf16(3, MAINS, span), bf16(3, SLOTS - MAINS, width),
        f32(pairs, 2 * SLOTS, 2 * hidden), bf16(pairs, SLOTS, 2 * hidden),
        f32(pairs, SLOTS, 2 * hidden), bf16(pairs, SLOTS, 2 * hidden),
        f32(SLOTS, width), f32(SLOTS, width),
    ]
    to_f, to_b = bf16(fines, MAINS, PIECE + LANE), bf16(pieces, MAINS, PIECE + LANE)
    scratch += [to_f, to_b, to_f, to_b]
    scratch += [bf16(tokens, width)] * 3 + [f32(1, width)]
    scratch += [f32(SLOTS, tokens)] * 4 + [f32(tokens, width)]
    scratch += [f32(1, width), f32(nz, 1, width), f32(1, width), f32(EXPERTS, 1, width)]
    scratch += [
        dma((8,)), dma((2,)), dma((last, nz - 1)), dma((last, nz - 1)),
        dma((3 * (EXPERTS - 1),)), dma((3 * (EXPERTS - 1),)),
        dma((fines, EXPERTS)), dma((fines, EXPERTS)), dma((pieces, EXPERTS)), dma((pieces, EXPERTS)),
        dma((6,)), dma((6,)),
        dma((EXPERTS - 1,)), dma((EXPERTS,)), dma((nz - 1,)), dma((nz,)),
    ]
    act, grad, gain_grad = pl.pallas_call(
        functools.partial(relay, (sections, nz, zlo)),
        out_shape=(
            jax.ShapeDtypeStruct((tokens, width), BF16),
            jax.ShapeDtypeStruct((tokens, width), BF16),
            jax.ShapeDtypeStruct((1, width), F32),
        ),
        in_specs=[hbm] * 10,
        out_specs=(vmem, vmem, vmem),
        scratch_shapes=scratch,
        compiler_params=pltpu.CompilerParams(
            collective_id=0, has_side_effects=True, vmem_limit_bytes=56 * 2**20
        ),
    )(
        x_fwd[0], gain, w_up[0], w_down[0], routes_f[0].T, probs_f[0].T,
        act_b[0], grad_b[0], routes_b[0].T, probs_b[0].T,
    )
    return act[None], grad[None], gain_grad


def solution(mesh):
    sizes = mesh.shape
    rows, weights = P("section", ("expert", "dp"), None), P("section", None, ("expert", "dp"))
    return jax.shard_map(
        functools.partial(body, sizes["section"], sizes["expert"], sizes["dp"]),
        mesh=mesh,
        in_specs=(rows, P("section", None), weights) + (rows,) * 7,
        out_specs=(rows, rows, P("section", None)),
        check_vma=False,
    )
```
